128 devices in a mesh: row: 16 (over z, x), rep: 8 (over y, core).
Axes of the slice: x: 4, y: 4, z: 4, core: 2. Of those that a mesh axis runs over, the one named last changes fastest.
Arguments:
- features: bfloat16 [65536, 256], P(('row', 'rep')), may hold values from -6 to 6
- weight: bfloat16 [256, 256], replicated, may hold values from -0.375 to 0.375
- cotangent: bfloat16 [65536, 256], P(('row', 'rep')), may hold values from -6 to 6
- row_mask: int32 [65536], P(('row', 'rep')), may hold values 0 or 1
- block_rows: int32 [49152], P(('row', 'rep')), may hold values from 0 to 31
- block_cols: int32 [49152], P(('row', 'rep')), may hold values from 0 to 63
- block_values: bfloat16 [49152, 128, 128], P(('row', 'rep')), may hold values from -0.06982422 to 0.06982422
- block_count: int32 [128], P(('row', 'rep')), may hold values from 48 to 384, as said below
Outputs:
- output: bfloat16 [65536, 256], P(('row', 'rep'))
- grad_features: bfloat16 [65536, 256], P(('row', 'rep'))
- grad_weight: float32 [256, 256], replicated
The draws below stay inside these ranges and needn't reach their ends.
Inputs may be any that keep to these rules, and one draw needn't show every extreme that they name: `block_count`: each device has at least one live slot; in every draw some device has all 384 slots live.
All inputs are finite; a program needn't handle non-finite values. No bound on the sum of `row_mask` on one device may be relied on, other than what follows from the above.
Results may differ from the reference program's by a relative error of at most 0.0061.
Values may be sent and summed in bfloat16 or wider, within the bound.
No kernel may reach another device: no remote copies, remote signals or barrier semaphores. Data moves between devices by JAX's collectives and lax.ppermute only.
A program may use at most 192 MiB of HBM per device.

```python
import math
import jax
import jax.numpy as jnp
from jax import lax

F = 256
BLOCK = 128
ROWS_DEV = 512
NNZ_DEV = 384
NODES = 65536
GROUP_ROWS = 4096
LINE_ROWS = 8192
SLOTS = 49152
N_REP = 8
DEVICES = 128


def draw_block_count(key, part):
    key = jax.random.fold_in(key, 7)
    first, second = jax.random.split(key)
    counts = jax.random.randint(first, (DEVICES,), max(1, NNZ_DEV // 8), NNZ_DEV + 1)
    busiest = jax.random.randint(second, (), 0, DEVICES)
    return jnp.where(jnp.arange(DEVICES) == busiest, NNZ_DEV, counts).astype(jnp.int32)


def place_ends(entries, key, low, high):
    longest = entries.shape.index(max(entries.shape))
    spots = []
    for shift in (0, 1):
        where = [jax.random.randint(jax.random.fold_in(key, axis), (), 0, length) for axis, length in enumerate(entries.shape)]
        where[longest] = (where[longest] + shift) % entries.shape[longest]
        spots.append(tuple(where))
    return entries.at[spots[0]].set(low).at[spots[1]].set(high)


def level_of(key, extent, shards, least, high):
    def one(position, parts):
        steps = jax.random.uniform(jax.random.fold_in(jax.random.fold_in(key, 6), position), (parts,), jnp.float32, least / len(shards), high / len(shards))
        return jnp.repeat(jnp.exp(steps), extent[position] // parts).reshape((-1,) + (1,) * (len(extent) - position - 1))

    factor_of = one(*shards[0])
    for cut in shards[1:]:
        factor_of = factor_of * one(*cut)
    return factor_of


def bell_draw(key, dims, spread, bound, cuts=(), kind=jnp.bfloat16):
    level = level_of(key, dims, cuts, -0.22, 0.18) if cuts else 1.0
    result = jax.random.normal(key, dims, jnp.float32) * spread * level
    return jnp.minimum(jnp.maximum(result, -bound), bound).astype(kind)


def setup_inputs(seed: int = 0) -> dict:
    seeds = jax.random.split(jax.random.key(seed), 9)
    features = bell_draw(seeds[0], (NODES, F), 1.0, 6.0, ((0, 128),))
    weight = bell_draw(seeds[1], (F, F), F ** -0.5, 0.375)
    cotangent = bell_draw(seeds[2], (NODES, F), 1.0, 6.0, ((0, 128),))
    row_mask = place_ends((jax.random.randint(seeds[3], (NODES,), 0, 2) < 1).astype(jnp.int32), jax.random.fold_in(seeds[3], 1), 0, 1)
    block_rows = place_ends(jax.random.randint(seeds[4], (SLOTS,), 0, GROUP_ROWS // BLOCK), jax.random.fold_in(seeds[4], 1), 0, (GROUP_ROWS // BLOCK) - 1).astype(jnp.int32)
    block_cols = place_ends(jax.random.randint(seeds[5], (SLOTS,), 0, LINE_ROWS // BLOCK), jax.random.fold_in(seeds[5], 1), 0, (LINE_ROWS // BLOCK) - 1).astype(jnp.int32)
    block_values = bell_draw(seeds[6], (SLOTS, BLOCK, BLOCK), 0.012, 0.06982422, ((0, 128),))
    block_count = draw_block_count(jax.random.fold_in(seeds[8], 71), 0)
    return dict(features=features, weight=weight, cotangent=cotangent, row_mask=row_mask, block_rows=block_rows, block_cols=block_cols, block_values=block_values, block_count=block_count)


def block_places(block_rows, block_cols, block_count):
    rows = block_rows.reshape(DEVICES, NNZ_DEV)
    cols = block_cols.reshape(DEVICES, NNZ_DEV)
    device = jnp.arange(DEVICES, dtype=jnp.int32)[:, None]
    group = device // N_REP
    rep_index = device % N_REP
    target = (group * (GROUP_ROWS // BLOCK) + rows).astype(jnp.int32)
    section = cols * BLOCK // ROWS_DEV
    within = cols * BLOCK % ROWS_DEV // BLOCK
    source = ((section * N_REP + rep_index) * (ROWS_DEV // BLOCK) + within).astype(jnp.int32)
    live = (jnp.arange(NNZ_DEV, dtype=jnp.int32)[None, :] < block_count[:, None]).astype(jnp.float32)
    return (target, source, live)

def reference(features, weight, cotangent, row_mask, block_rows, block_cols, block_values, block_count):
    target, source, live = block_places(block_rows, block_cols, block_count)
    values = block_values.reshape(DEVICES, NNZ_DEV, BLOCK, BLOCK)
    feature_blocks = features.reshape(NODES // BLOCK, BLOCK, F)

    def forward_step(total, item):
        vals, tgt, src, lv = item
        product = jnp.einsum('kab,kbf->kaf', vals.astype(jnp.float32), feature_blocks[src].astype(jnp.float32))
        return (total.at[tgt].add(product * lv[:, None, None]), None)
    start = jnp.zeros((NODES // BLOCK, BLOCK, F), jnp.float32)
    total, _ = lax.scan(forward_step, start, (values, target, source, live))
    aggregated = total.reshape(NODES, F).astype(jnp.bfloat16)
    pre = jnp.dot(aggregated, weight, preferred_element_type=jnp.float32)
    gate = jax.nn.sigmoid(pre)
    output = (pre * gate).astype(jnp.bfloat16)
    mask = row_mask.astype(jnp.float32)[:, None]
    slope = (cotangent.astype(jnp.float32) * mask * gate * (1.0 + pre * (1.0 - gate))).astype(jnp.bfloat16)
    grad_weight = lax.dot_general(aggregated, slope, (((0,), (0,)), ((), ())), preferred_element_type=jnp.float32) * (1.0 / math.sqrt(NODES))
    back = jnp.dot(slope, weight.T, preferred_element_type=jnp.float32).astype(jnp.bfloat16)
    back_blocks = back.reshape(NODES // BLOCK, BLOCK, F)

    def backward_step(total, item):
        vals, tgt, src, lv = item
        product = jnp.einsum('kab,kaf->kbf', vals.astype(jnp.float32), back_blocks[tgt].astype(jnp.float32))
        return (total.at[src].add(product * lv[:, None, None]), None)
    total_back, _ = lax.scan(backward_step, jnp.zeros((NODES // BLOCK, BLOCK, F), jnp.float32), (values, target, source, live))
    grad_features = total_back.reshape(NODES, F).astype(jnp.bfloat16)
    return (output, grad_features, grad_weight)
```

```python
import functools
import math

import jax
import jax.numpy as jnp
from jax import lax
from jax.experimental import pallas as pl
from jax.experimental.pallas import tpu as pltpu
from jax.sharding import PartitionSpec as P

EDGE = 128
MIB = 2**20


def spmm_body(per, unroll, n_dst, dims, count, src_idx, dst_idx, values, src, out, acc):
    i = pl.program_id(0)
    n = count[0]

    @pl.when(i == 0)
    def _():
        acc[...] = jnp.zeros_like(acc)

    @pl.when(i * per < n)
    def _():
        def one(k):
            g = i * per + k
            s = src_idx[g]
            d = jnp.where(g < n, dst_idx[g], n_dst)
            x = src[pl.ds(pl.multiple_of(s * EDGE, EDGE), EDGE), :]
            p = lax.dot_general(values[k], x, (dims, ((), ())), preferred_element_type=jnp.float32)
            acc[pl.ds(pl.multiple_of(d * EDGE, EDGE), EDGE), :] += p

        def step(t, carry):
            for u in range(unroll):
                one(t * unroll + u)
            return carry

        lax.fori_loop(0, per // unroll, step, 0)

    @pl.when(i == pl.num_programs(0) - 1)
    def _():
        out[...] = acc[: n_dst * EDGE, :].astype(out.dtype)


def spmm(count, src_idx, dst_idx, values, src, n_dst, transposed):
    slots = values.shape[0]
    width = src.shape[1]
    per = math.gcd(slots, 32)
    unroll = math.gcd(per, 8)
    dims = ((0,), (0,)) if transposed else ((1,), (0,))

    def chunk(i, count, s, d):
        return (jnp.minimum(i, jnp.maximum(count[0] - 1, 0) // per), 0, 0)

    whole = lambda i, *_: (0, 0)
    return pl.pallas_call(
        functools.partial(spmm_body, per, unroll, n_dst, dims),
        grid_spec=pltpu.PrefetchScalarGridSpec(
            num_scalar_prefetch=3,
            grid=(slots // per,),
            in_specs=[
                pl.BlockSpec((per, EDGE, EDGE), chunk),
                pl.BlockSpec(src.shape, whole),
            ],
            out_specs=pl.BlockSpec((n_dst * EDGE, width), whole),
            scratch_shapes=[pltpu.VMEM(((n_dst + 1) * EDGE, width), jnp.float32)],
        ),
        out_shape=jax.ShapeDtypeStruct((n_dst * EDGE, width), jnp.bfloat16),
        compiler_params=pltpu.CompilerParams(vmem_limit_bytes=48 * MIB),
    )(count, src_idx, dst_idx, values, src)


def shards(
    features, weight, cotangent, row_mask, block_rows, block_cols, block_values, block_count
):
    rows_dev, width = features.shape
    n_rep = lax.axis_size("rep")
    n_row = lax.axis_size("row")
    factor = 1.0 / math.sqrt(rows_dev * n_row * n_rep)
    group_blocks = n_rep * rows_dev // EDGE
    line_blocks = n_row * rows_dev // EDGE

    line = lax.all_gather(features, "row", axis=0, tiled=True)
    partial_value = spmm(
        block_count, block_cols, block_rows, block_values, line, group_blocks, False
    )
    parts = lax.all_to_all(partial_value, "rep", 0, 0, tiled=True)
    summed = jnp.sum(parts.reshape(n_rep, rows_dev, width).astype(jnp.float32), axis=0)
    aggregated = summed.astype(jnp.bfloat16)
    pre = jnp.dot(aggregated, weight, preferred_element_type=jnp.float32)
    gate = jax.nn.sigmoid(pre)
    output = (pre * gate).astype(jnp.bfloat16)
    mask = row_mask.astype(jnp.float32)[:, None]
    slope = (cotangent.astype(jnp.float32) * mask * gate * (1.0 + pre * (1.0 - gate))).astype(
        jnp.bfloat16
    )
    weight_term = lax.dot_general(
        aggregated, slope, (((0,), (0,)), ((), ())), preferred_element_type=jnp.float32
    )
    grad_weight = lax.psum(weight_term, ("row", "rep")) * factor
    own_back = jnp.dot(slope, weight.T, preferred_element_type=jnp.float32).astype(jnp.bfloat16)
    group_back = lax.all_gather(own_back, "rep", axis=0, tiled=True)
    line_total = spmm(
        block_count, block_rows, block_cols, block_values, group_back, line_blocks, True
    )
    line_parts = lax.all_to_all(line_total, "row", 0, 0, tiled=True)
    grad_features = jnp.sum(
        line_parts.reshape(n_row, rows_dev, width).astype(jnp.float32), axis=0
    ).astype(jnp.bfloat16)
    return (output, grad_features, grad_weight)


def solution(mesh):
    in_specs = (
        P(("row", "rep"), None),
        P(),
        P(("row", "rep"), None),
        P(("row", "rep")),
        P(("row", "rep")),
        P(("row", "rep")),
        P(("row", "rep"), None, None),
        P(("row", "rep")),
    )
    out_specs = (P(("row", "rep"), None), P(("row", "rep"), None), P())
    return jax.shard_map(shards, mesh=mesh, in_specs=in_specs, out_specs=out_specs, check_vma=False)
```

```python
import functools
import math

import jax
import jax.numpy as jnp
from jax import lax
from jax.experimental import pallas as pl
from jax.experimental.pallas import tpu as pltpu
from jax.sharding import PartitionSpec as P

EDGE = 128
MIB = 2**20
RING = 4
CORES = 2
UNROLL = 8
DEPTH = 4

f32 = jnp.float32
bf16 = jnp.bfloat16


def spmm_body(transposed, splits, n_src, steps, slots, srcs, dsts, values, *refs):
    pieces, rest = refs[:n_src], refs[n_src:]
    outs, (src, acc, ring, src_sem, sems) = rest[: len(splits)], rest[len(splits) :]
    n_steps = steps[0]

    def fetch(step, bank):
        for u in range(UNROLL):
            pair = step * UNROLL + u
            for half in range(2):
                place = pl.ds(half * EDGE, EDGE)
                at = ring.at[bank, u, place, :] if transposed else ring.at[bank, u, :, place]
                pltpu.make_async_copy(values.at[slots[2 * pair + half]], at, sems.at[bank]).start()

    for ahead in range(DEPTH - 1):

        @pl.when(ahead < n_steps)
        def _():
            fetch(ahead, ahead)

    base = 0
    for piece in pieces:
        rows = piece.shape[0]
        pltpu.make_async_copy(piece, src.at[pl.ds(base, rows), :], src_sem).start()
        base += rows
    src[pl.ds(base, EDGE), :] = jnp.zeros((EDGE, src.shape[1]), src.dtype)
    acc[...] = jnp.zeros_like(acc)
    loaded = src.at[pl.ds(0, base), :]
    pltpu.make_async_copy(loaded, loaded, src_sem).wait()
    dims = (((0,), (0,)), ((), ())) if transposed else (((1,), (0,)), ((), ()))

    def step(t, carry):
        bank = lax.rem(t, DEPTH)

        ahead = t + DEPTH - 1

        @pl.when(ahead < n_steps)
        def _():
            fetch(ahead, lax.rem(ahead, DEPTH))

        pltpu.make_async_copy(ring.at[bank], ring.at[bank], sems.at[bank]).wait()
        for u in range(UNROLL):
            pair = t * UNROLL + u
            x = jnp.concatenate(
                [
                    src[pl.ds(pl.multiple_of(srcs[2 * pair + half] * EDGE, EDGE), EDGE), :]
                    for half in range(2)
                ],
                axis=0,
            )
            product = lax.dot_general(ring[bank, u], x, dims, preferred_element_type=f32)
            acc[pl.ds(pl.multiple_of(dsts[pair] * EDGE, EDGE), EDGE), :] += product
        return carry

    lax.fori_loop(0, n_steps, step, 0)
    base = 0
    for out in outs:
        rows = out.shape[0]
        out[...] = acc[pl.ds(base, rows), :].astype(out.dtype)
        base += rows


def spmm(lists, values, pieces, splits, transposed):
    steps, slots, srcs, dsts = lists
    width = pieces[0].shape[1]
    n_src = sum(p.shape[0] for p in pieces)
    n_dst = sum(rows for rows, _ in splits)
    bank = (UNROLL, 2 * EDGE, EDGE) if transposed else (UNROLL, EDGE, 2 * EDGE)
    smem = pl.BlockSpec(memory_space=pltpu.SMEM)
    anywhere = pl.BlockSpec(memory_space=pl.ANY)
    vmem = pl.BlockSpec(memory_space=pltpu.VMEM)
    return pl.pallas_call(
        functools.partial(spmm_body, transposed, splits, len(pieces)),
        in_specs=[smem] * 4 + [anywhere] * (1 + len(pieces)),
        out_specs=[vmem] * len(splits),
        out_shape=[jax.ShapeDtypeStruct((rows, width), kind) for rows, kind in splits],
        scratch_shapes=[
            pltpu.VMEM((n_src + EDGE, width), bf16),
            pltpu.VMEM((n_dst, width), f32),
            pltpu.VMEM((DEPTH, *bank), bf16),
            pltpu.SemaphoreType.DMA,
            pltpu.SemaphoreType.DMA((DEPTH,)),
        ],
        compiler_params=pltpu.CompilerParams(vmem_limit_bytes=54 * MIB),
        cost_estimate=pl.CostEstimate(
            flops=values.shape[0] * EDGE * EDGE * width,
            bytes_accessed=values.shape[0] * EDGE * EDGE,
            transcendentals=0,
        ),
    )(steps, slots, srcs, dsts, values, *pieces)


def pair_lists(live, dst, src, n_dst, n_src):
    slots = dst.shape[0]
    room = -(-((slots + n_dst) // 2) // UNROLL) * UNROLL
    index = jnp.arange(slots, dtype=jnp.int32)
    same = (dst[:, None] == dst[None, :]) & live[None, :]
    rank = jnp.sum((same & (index[None, :] < index[:, None])).astype(jnp.int32), axis=1)
    bins = jnp.arange(n_dst, dtype=jnp.int32)
    counts = jnp.sum(((dst[:, None] == bins[None, :]) & live[:, None]).astype(jnp.int32), axis=0)
    pairs = (counts + 1) // 2
    start = jnp.sum(jnp.where(bins[None, :] < dst[:, None], pairs[None, :], 0), axis=1)
    place = jnp.where(live, 2 * start + rank, -1)
    places = jnp.arange(2 * room, dtype=jnp.int32)
    hit = place[None, :] == places[:, None]
    slot_at = jnp.sum(jnp.where(hit, index[None, :], 0), axis=1)
    src_at = n_src + jnp.sum(jnp.where(hit, src[None, :] - n_src, 0), axis=1)
    dst_at = jnp.sum(jnp.where(hit, dst[None, :], 0), axis=1)[::2]
    steps = (jnp.sum(pairs) + UNROLL - 1) // UNROLL
    return steps.reshape(1), slot_at, src_at, dst_at


def from_ring(value, axis, stride, size, shift):
    pairs = []
    for i in range(size):
        at = i // stride % RING
        pairs.append((i + ((at + shift) % RING - at) * stride, i))
    return lax.ppermute(value, axis, pairs)


def other_core(value):
    return lax.ppermute(value, "rep", [(i, i ^ 1) for i in range(RING * CORES)])


def shards(
    features, weight, cotangent, row_mask, block_rows, block_cols, block_values, block_count
):
    rows_dev, width = features.shape
    n_rep = lax.axis_size("rep")
    n_row = lax.axis_size("row")
    factor = 1.0 / math.sqrt(rows_dev * n_row * n_rep)
    group_blocks = n_rep * rows_dev // EDGE
    line_blocks = n_row * rows_dev // EDGE
    half_rows = rows_dev // 2
    per_half = half_rows // EDGE
    per_dev = rows_dev // EDGE
    i, j = lax.axis_index("row"), lax.axis_index("rep")
    z, x, y, core = i // RING, i % RING, j // CORES, j % CORES
    ring_x = functools.partial(from_ring, axis="row", stride=1, size=n_row)
    ring_z = functools.partial(from_ring, axis="row", stride=RING, size=n_row)
    ring_y = functools.partial(from_ring, axis="rep", stride=CORES, size=n_rep)
    shifts = (1, 3, 2)

    def gather(value, ring):
        got = {s: ring(value, shift=s) for s in shifts}
        return [value, got[1], got[2], got[3]]

    first, second = features[:half_rows], features[half_rows:]
    first_x, second_z = gather(first, ring_x), gather(second, ring_z)
    line = gather(jnp.concatenate(first_x), ring_z) + gather(jnp.concatenate(second_z), ring_x)

    live = jnp.arange(block_rows.shape[0], dtype=jnp.int32) < block_count[0]
    dev, q = block_rows // per_dev, block_rows % per_dev
    dy = (dev // CORES - y) % RING
    across = (dev % CORES) ^ core
    row_at = (across * RING + dy) * per_dev + q
    dev, q = block_cols // per_dev, block_cols % per_dev
    dz, dx = (dev // RING - z) % RING, (dev % RING - x) % RING
    h = q // per_half
    zx, xz = dz * RING + dx, dx * RING + dz
    gathered_at = (h * n_row + jnp.where(h == 0, zx, xz)) * per_half + q % per_half
    scattered_at = (h * n_row + jnp.where(h == 0, xz, zx)) * per_half + q % per_half
    forward = pair_lists(live, row_at, gathered_at, group_blocks, line_blocks)
    backward = pair_lists(live, scattered_at, row_at, line_blocks, group_blocks)
    line, forward, backward = lax.optimization_barrier((line, forward, backward))

    def scatter(parts, ring):
        got = {s: ring(parts[s], shift=RING - s) for s in shifts}
        return parts[0] + got[1].astype(f32) + got[2].astype(f32) + got[3].astype(f32)

    def cut(value, rows):
        return [value[k * rows : (k + 1) * rows] for k in range(RING)]

    side = RING * rows_dev
    mine, others = spmm(forward, block_values, line, ((side, f32), (side, bf16)), False)
    others = other_core(others)
    chip = [a + b.astype(f32) for a, b in zip(cut(mine, rows_dev), cut(others, rows_dev))]
    summed = scatter(chip[:1] + [c.astype(bf16) for c in chip[1:]], ring_y)
    aggregated = summed.astype(bf16)
    pre = jnp.dot(aggregated, weight, preferred_element_type=f32)
    gate = jax.nn.sigmoid(pre)
    output = (pre * gate).astype(bf16)
    mask = row_mask.astype(f32)[:, None]
    slope = (cotangent.astype(f32) * mask * gate * (1.0 + pre * (1.0 - gate))).astype(bf16)
    back = jnp.dot(slope, weight.T, preferred_element_type=f32).astype(bf16)
    backs = gather(back, ring_y)

    weight_term = lax.dot_general(
        aggregated, slope, (((0,), (0,)), ((), ())), preferred_element_type=f32
    )
    weight_term, backs[1] = lax.optimization_barrier((weight_term, backs[1]))
    backs += [other_core(jnp.concatenate(backs))]
    strip = weight_term.shape[0] // n_rep
    strips = weight_term.reshape(RING, CORES, strip, width)

    def at_ring(s):
        return lax.dynamic_index_in_dim(strips, (y + s) % RING, 0, keepdims=False)

    pair = scatter([at_ring(s) for s in range(RING)], ring_y)
    kept = jnp.where(core == 0, pair[0], pair[1])
    own = kept + other_core(jnp.where(core == 0, pair[1], pair[0]))

    ring_rows = RING * half_rows
    splits = (((ring_rows, f32),) + ((ring_rows, bf16),) * (RING - 1)) * 2
    parts = spmm(backward, block_values, backs, splits, True)

    def send(parts, ring):
        return {s: ring(parts[s], shift=RING - s) for s in shifts}

    def add(own, got):
        return own + got[1].astype(f32) + got[2].astype(f32) + got[3].astype(f32)

    near_got = [send(parts[:RING], ring_x), send(parts[RING:], ring_z)]
    own, near_got[0][1] = lax.optimization_barrier((own, near_got[0][1]))
    strips = lax.all_to_all(
        jnp.broadcast_to(own[None], (n_row, strip, width)), "row", 0, 0, tiled=True
    )
    strips = jnp.broadcast_to(jnp.sum(strips, axis=0)[None] * factor, (n_rep, strip, width))
    grad_weight = lax.all_to_all(strips, "rep", 0, 0, tiled=True).reshape(-1, width)
    near_sums = [
        cut(add(own, got), half_rows) for own, got in zip((parts[0], parts[RING]), near_got)
    ]
    totals = [
        scatter(near[:1] + [c.astype(bf16) for c in near[1:]], far)
        for near, far in zip(near_sums, (ring_z, ring_x))
    ]
    grad_features = jnp.concatenate(totals).astype(bf16)
    return output, grad_features, grad_weight


def solution(mesh):
    in_specs = (
        P(("row", "rep"), None),
        P(),
        P(("row", "rep"), None),
        P(("row", "rep")),
        P(("row", "rep")),
        P(("row", "rep")),
        P(("row", "rep"), None, None),
        P(("row", "rep")),
    )
    out_specs = (P(("row", "rep"), None), P(("row", "rep"), None), P())
    return jax.shard_map(shards, mesh=mesh, in_specs=in_specs, out_specs=out_specs, check_vma=False)
```

```python
import functools
import math

import jax
import jax.numpy as jnp
from jax import lax
from jax.experimental import pallas as pl
from jax.experimental.pallas import tpu as pltpu
from jax.sharding import PartitionSpec as P

EDGE = 128
MIB = 2**20
RING = 4
CORES = 2
UNROLL = 16
DEPTH = 4

f32 = jnp.float32
bf16 = jnp.bfloat16


def spmm_body(transposed, splits, n_src, room, table, values, *refs):
    pieces, rest = refs[:n_src], refs[n_src:]
    outs, (src, acc, narrow, ring, src_sem, out_sem, sems) = rest[: len(splits)], rest[len(splits) :]
    n_steps = table[5 * room]

    def fetch(step, bank):
        for u in range(UNROLL):
            pair = step * UNROLL + u
            for half in range(2):
                place = pl.ds(half * EDGE, EDGE)
                at = ring.at[bank, u, place, :] if transposed else ring.at[bank, u, :, place]
                pltpu.make_async_copy(values.at[table[2 * pair + half]], at, sems.at[bank]).start()

    for ahead in range(DEPTH - 1):

        @pl.when(ahead < n_steps)
        def _():
            fetch(ahead, ahead)

    base = 0
    for piece in pieces:
        rows = piece.shape[0]
        pltpu.make_async_copy(piece, src.at[pl.ds(base, rows), :], src_sem).start()
        base += rows
    src[pl.ds(base, EDGE), :] = jnp.zeros((EDGE, src.shape[1]), src.dtype)
    acc[...] = jnp.zeros_like(acc)
    loaded = src.at[pl.ds(0, base), :]
    pltpu.make_async_copy(loaded, loaded, src_sem).wait()
    dims = (((0,), (0,)), ((), ())) if transposed else (((1,), (0,)), ((), ()))

    def step(t, carry):
        bank = lax.rem(t, DEPTH)
        ahead = t + DEPTH - 1

        @pl.when(ahead < n_steps)
        def _():
            fetch(ahead, lax.rem(ahead, DEPTH))

        pltpu.make_async_copy(ring.at[bank], ring.at[bank], sems.at[bank]).wait()
        for u in range(UNROLL):
            pair = t * UNROLL + u
            x = jnp.concatenate(
                [
                    src[pl.ds(pl.multiple_of(table[2 * (room + pair) + half] * EDGE, EDGE), EDGE), :]
                    for half in range(2)
                ],
                axis=0,
            )
            product = lax.dot_general(ring[bank, u], x, dims, preferred_element_type=f32)
            acc[pl.ds(pl.multiple_of(table[4 * room + pair] * EDGE, EDGE), EDGE), :] += product
        return carry

    lax.fori_loop(0, n_steps, step, 0)
    base = 0
    for out in outs:
        rows = out.shape[0]
        at = acc.at[pl.ds(base, rows), :]
        if out.dtype != acc.dtype:
            narrow[pl.ds(base, rows), :] = acc[pl.ds(base, rows), :].astype(out.dtype)
            at = narrow.at[pl.ds(base, rows), :]
        pltpu.make_async_copy(at, out, out_sem).start()
        base += rows
    for out in outs:
        pltpu.make_async_copy(out, out, out_sem).wait()


def spmm(table, values, pieces, splits, transposed):
    width = pieces[0].shape[1]
    n_src = sum(p.shape[0] for p in pieces)
    n_dst = sum(rows for rows, _ in splits)
    bank = (UNROLL, 2 * EDGE, EDGE) if transposed else (UNROLL, EDGE, 2 * EDGE)
    smem = pl.BlockSpec(memory_space=pltpu.SMEM)
    anywhere = pl.BlockSpec(memory_space=pl.ANY)
    return pl.pallas_call(
        functools.partial(spmm_body, transposed, splits, len(pieces), table.shape[0] // 5),
        in_specs=[smem] + [anywhere] * (1 + len(pieces)),
        out_specs=[anywhere] * len(splits),
        out_shape=[jax.ShapeDtypeStruct((rows, width), kind) for rows, kind in splits],
        scratch_shapes=[
            pltpu.VMEM((n_src + EDGE, width), bf16),
            pltpu.VMEM((n_dst, width), f32),
            pltpu.VMEM((n_dst, width), bf16),
            pltpu.VMEM((DEPTH, *bank), bf16),
            pltpu.SemaphoreType.DMA,
            pltpu.SemaphoreType.DMA,
            pltpu.SemaphoreType.DMA((DEPTH,)),
        ],
        compiler_params=pltpu.CompilerParams(vmem_limit_bytes=54 * MIB),
        cost_estimate=pl.CostEstimate(
            flops=2 * values.shape[0] * EDGE * EDGE * width,
            bytes_accessed=2 * values.shape[0] * EDGE * EDGE,
            transcendentals=0,
        ),
    )(table, values, *pieces)


def pair_lists(live, dst, src, n_dst, n_src):
    slots = dst.shape[0]
    room = -(-((slots + n_dst) // 2) // UNROLL) * UNROLL
    index = jnp.arange(slots, dtype=jnp.int32)
    same = (dst[:, None] == dst[None, :]) & live[None, :]
    rank = jnp.sum((same & (index[None, :] < index[:, None])).astype(jnp.int32), axis=1)
    bins = jnp.arange(n_dst, dtype=jnp.int32)
    counts = jnp.sum(((dst[:, None] == bins[None, :]) & live[:, None]).astype(jnp.int32), axis=0)
    pairs = (counts + 1) // 2
    start = jnp.sum(jnp.where(bins[None, :] < dst[:, None], pairs[None, :], 0), axis=1)
    place = jnp.where(live, 2 * start + rank, -1)
    places = jnp.arange(2 * room, dtype=jnp.int32)
    hit = place[None, :] == places[:, None]
    slot_at = jnp.sum(jnp.where(hit, index[None, :], 0), axis=1)
    src_at = n_src + jnp.sum(jnp.where(hit, src[None, :] - n_src, 0), axis=1)
    dst_at = jnp.sum(jnp.where(hit, dst[None, :], 0), axis=1)[::2]
    steps = (jnp.sum(pairs) + UNROLL - 1) // UNROLL
    return jnp.concatenate([slot_at, src_at, dst_at, steps.reshape(1)])


def from_ring(value, axis, stride, size, shift):
    pairs = []
    for i in range(size):
        at = i // stride % RING
        pairs.append((i + ((at + shift) % RING - at) * stride, i))
    return lax.ppermute(value, axis, pairs)


def other_core(value):
    return lax.ppermute(value, "rep", [(i, i ^ 1) for i in range(RING * CORES)])


def shards(
    features, weight, cotangent, row_mask, block_rows, block_cols, block_values, block_count
):
    rows_dev, width = features.shape
    n_rep = lax.axis_size("rep")
    n_row = lax.axis_size("row")
    factor = 1.0 / math.sqrt(rows_dev * n_row * n_rep)
    group_blocks = n_rep * rows_dev // EDGE
    line_blocks = n_row * rows_dev // EDGE
    half_rows = rows_dev // 2
    per_half = half_rows // EDGE
    per_dev = rows_dev // EDGE
    i, j = lax.axis_index("row"), lax.axis_index("rep")
    z, x, y, core = i // RING, i % RING, j // CORES, j % CORES
    ring_x = functools.partial(from_ring, axis="row", stride=1, size=n_row)
    ring_z = functools.partial(from_ring, axis="row", stride=RING, size=n_row)
    ring_y = functools.partial(from_ring, axis="rep", stride=CORES, size=n_rep)
    shifts = (1, 3, 2)

    def gather(value, ring):
        got = {s: ring(value, shift=s) for s in shifts}
        return [value, got[1], got[2], got[3]]

    first, second = features[:half_rows], features[half_rows:]
    first_x, second_z = gather(first, ring_x), gather(second, ring_z)
    second_z = jnp.concatenate(second_z)
    middle = second_z.shape[0] // 2
    up, down = ring_x(second_z, shift=1), ring_x(second_z, shift=3)
    across_up, across_down = ring_x(up[:middle], shift=1), ring_x(down[middle:], shift=3)
    line = gather(jnp.concatenate(first_x), ring_z)
    line += [second_z, up, across_up, across_down, down]

    live = jnp.arange(block_rows.shape[0], dtype=jnp.int32) < block_count[0]
    dev, q = block_rows // per_dev, block_rows % per_dev
    dy = (dev // CORES - y) % RING
    across = (dev % CORES) ^ core
    row_at = (across * RING + dy) * per_dev + q
    dev, q = block_cols // per_dev, block_cols % per_dev
    dz, dx = (dev // RING - z) % RING, (dev % RING - x) % RING
    h = q // per_half
    zx, xz = dz * RING + dx, dx * RING + dz
    gathered_at = (h * n_row + jnp.where(h == 0, zx, xz)) * per_half + q % per_half
    scattered_at = (h * n_row + jnp.where(h == 0, xz, zx)) * per_half + q % per_half
    forward = pair_lists(live, row_at, gathered_at, group_blocks, line_blocks)
    backward = pair_lists(live, scattered_at, row_at, line_blocks, group_blocks)
    line, forward, backward = lax.optimization_barrier((line, forward, backward))

    def scatter(parts, ring):
        got = {s: ring(parts[s], shift=RING - s) for s in shifts}
        return parts[0] + got[1].astype(f32) + got[2].astype(f32) + got[3].astype(f32)

    def cut(value, rows):
        return [value[k * rows : (k + 1) * rows] for k in range(RING)]

    side = RING * rows_dev
    mine, others = spmm(forward, block_values, line, ((side, f32), (side, bf16)), False)
    others = other_core(others)
    chip = [a + b.astype(f32) for a, b in zip(cut(mine, rows_dev), cut(others, rows_dev))]
    summed = scatter(chip[:1] + [c.astype(bf16) for c in chip[1:]], ring_y)
    aggregated = summed.astype(bf16)
    pre = jnp.dot(aggregated, weight, preferred_element_type=f32)
    gate = jax.nn.sigmoid(pre)
    output = (pre * gate).astype(bf16)
    mask = row_mask.astype(f32)[:, None]
    slope = (cotangent.astype(f32) * mask * gate * (1.0 + pre * (1.0 - gate))).astype(bf16)
    back = jnp.dot(slope, weight.T, preferred_element_type=f32).astype(bf16)
    backs = gather(back, ring_y)

    backs += [other_core(jnp.concatenate(backs))]

    weight_term = lax.dot_general(
        aggregated, slope, (((0,), (0,)), ((), ())), preferred_element_type=f32
    )
    devices = n_row * n_rep
    strips = lax.all_to_all(
        weight_term.reshape(devices, -1, width), ("row", "rep"), 0, 0, tiled=True
    )

    ring_rows = RING * half_rows
    part_rows = ring_rows // 2
    splits = ((ring_rows, f32),) + ((ring_rows, bf16),) * (RING - 1)
    splits += ((ring_rows, f32), (part_rows, f32), (part_rows, bf16), (part_rows, bf16))
    splits += ((part_rows, bf16), (part_rows, bf16), (part_rows, f32))
    parts = spmm(backward, block_values, backs, splits, True)
    parts, strips = lax.optimization_barrier((parts, strips))
    strip = jnp.sum(strips, axis=0) * factor

    def send(parts, ring):
        return {s: ring(parts[s], shift=RING - s) for s in shifts}

    def add(own, got):
        return own + got[1].astype(f32) + got[2].astype(f32) + got[3].astype(f32)

    near_first = send(parts[:RING], ring_x)
    own_z, up_a, up_b, across_a, across_b, down_a, down_b = parts[RING:]
    through_a, through_b = ring_z(across_a, shift=3), ring_z(across_b, shift=1)
    up = jnp.concatenate([(up_a + through_a.astype(f32)).astype(bf16), up_b])
    down = jnp.concatenate([down_a, (down_b + through_b.astype(f32)).astype(bf16)])

    up, down, strip = lax.optimization_barrier((up, down, strip))
    from_up, from_down = ring_z(up, shift=3), ring_z(down, shift=1)
    grad_weight = lax.all_to_all(
        jnp.broadcast_to(strip[None], strips.shape), ("row", "rep"), 0, 0, tiled=True
    ).reshape(-1, width)

    near_sum = cut(add(parts[0], near_first), half_rows)
    far_first = near_sum[:1] + [c.astype(bf16) for c in near_sum[1:]]
    far_first_got = send(far_first, ring_z)
    near_sum = cut(own_z + from_up.astype(f32) + from_down.astype(f32), half_rows)
    far_second = near_sum[:1] + [c.astype(bf16) for c in near_sum[1:]]
    far_second_got = send(far_second, ring_x)
    totals = [add(far_first[0], far_first_got), add(far_second[0], far_second_got)]
    grad_features = jnp.concatenate(totals).astype(bf16)
    return output, grad_features, grad_weight


def solution(mesh):
    in_specs = (
        P(("row", "rep"), None),
        P(),
        P(("row", "rep"), None),
        P(("row", "rep")),
        P(("row", "rep")),
        P(("row", "rep")),
        P(("row", "rep"), None, None),
        P(("row", "rep")),
    )
    out_specs = (P(("row", "rep"), None), P(("row", "rep"), None), P())
    return jax.shard_map(shards, mesh=mesh, in_specs=in_specs, out_specs=out_specs, check_vma=False)
```

```python
import functools
import math

import jax
import jax.numpy as jnp
from jax import lax
from jax.experimental import pallas as pl
from jax.experimental.pallas import tpu as pltpu
from jax.sharding import PartitionSpec as P

EDGE = 128
MIB = 2**20
RING = 4
CORES = 2
UNROLL = 16
DEPTH = 4

f32 = jnp.float32
bf16 = jnp.bfloat16


def spmm_body(transposed, splits, n_src, room, table, values, *refs):
    pieces, rest = refs[:n_src], refs[n_src:]
    outs, (src, acc, narrow, ring, src_sem, out_sem, sems) = rest[: len(splits)], rest[len(splits) :]
    n_steps = table[5 * room]

    def fetch(step, bank):
        for u in range(UNROLL):
            pair = step * UNROLL + u
            for half in range(2):
                place = pl.ds(half * EDGE, EDGE)
                at = ring.at[bank, u, place, :] if transposed else ring.at[bank, u, :, place]
                pltpu.make_async_copy(values.at[table[2 * pair + half]], at, sems.at[bank]).start()

    for ahead in range(DEPTH - 1):

        @pl.when(ahead < n_steps)
        def _():
            fetch(ahead, ahead)

    base = 0
    for piece in pieces:
        rows = piece.shape[0]
        pltpu.make_async_copy(piece, src.at[pl.ds(base, rows), :], src_sem).start()
        base += rows
    src[pl.ds(base, EDGE), :] = jnp.zeros((EDGE, src.shape[1]), src.dtype)
    acc[...] = jnp.zeros_like(acc)
    loaded = src.at[pl.ds(0, base), :]
    pltpu.make_async_copy(loaded, loaded, src_sem).wait()
    dims = (((0,), (0,)), ((), ())) if transposed else (((1,), (0,)), ((), ()))

    def step(t, carry):
        bank = lax.rem(t, DEPTH)
        ahead = t + DEPTH - 1

        @pl.when(ahead < n_steps)
        def _():
            fetch(ahead, lax.rem(ahead, DEPTH))

        pltpu.make_async_copy(ring.at[bank], ring.at[bank], sems.at[bank]).wait()
        for u in range(UNROLL):
            pair = t * UNROLL + u
            x = jnp.concatenate(
                [
                    src[pl.ds(pl.multiple_of(table[2 * (room + pair) + half] * EDGE, EDGE), EDGE), :]
                    for half in range(2)
                ],
                axis=0,
            )
            product = lax.dot_general(ring[bank, u], x, dims, preferred_element_type=f32)
            acc[pl.ds(pl.multiple_of(table[4 * room + pair] * EDGE, EDGE), EDGE), :] += product
        return carry

    lax.fori_loop(0, n_steps, step, 0)
    base = 0
    for out in outs:
        rows = out.shape[0]
        at = acc.at[pl.ds(base, rows), :]
        if out.dtype != acc.dtype:
            narrow[pl.ds(base, rows), :] = acc[pl.ds(base, rows), :].astype(out.dtype)
            at = narrow.at[pl.ds(base, rows), :]
        pltpu.make_async_copy(at, out, out_sem).start()
        base += rows
    for out in outs:
        pltpu.make_async_copy(out, out, out_sem).wait()


def spmm(table, values, pieces, splits, transposed):
    width = pieces[0].shape[1]
    n_src = sum(p.shape[0] for p in pieces)
    n_dst = sum(rows for rows, _ in splits)
    bank = (UNROLL, 2 * EDGE, EDGE) if transposed else (UNROLL, EDGE, 2 * EDGE)
    smem = pl.BlockSpec(memory_space=pltpu.SMEM)
    anywhere = pl.BlockSpec(memory_space=pl.ANY)
    return pl.pallas_call(
        functools.partial(spmm_body, transposed, splits, len(pieces), table.shape[0] // 5),
        in_specs=[smem] + [anywhere] * (1 + len(pieces)),
        out_specs=[anywhere] * len(splits),
        out_shape=[jax.ShapeDtypeStruct((rows, width), kind) for rows, kind in splits],
        scratch_shapes=[
            pltpu.VMEM((n_src + EDGE, width), bf16),
            pltpu.VMEM((n_dst, width), f32),
            pltpu.VMEM((n_dst, width), bf16),
            pltpu.VMEM((DEPTH, *bank), bf16),
            pltpu.SemaphoreType.DMA,
            pltpu.SemaphoreType.DMA,
            pltpu.SemaphoreType.DMA((DEPTH,)),
        ],
        compiler_params=pltpu.CompilerParams(vmem_limit_bytes=49 * MIB),
        cost_estimate=pl.CostEstimate(
            flops=2 * values.shape[0] * EDGE * EDGE * width,
            bytes_accessed=2 * values.shape[0] * EDGE * EDGE,
            transcendentals=0,
        ),
    )(table, values, *pieces)


def pair_lists(live, dst, src, n_dst, n_src):
    slots = dst.shape[0]
    room = -(-((slots + n_dst) // 2) // UNROLL) * UNROLL
    index = jnp.arange(slots, dtype=jnp.int32)
    same = (dst[:, None] == dst[None, :]) & live[None, :]
    rank = jnp.sum((same & (index[None, :] < index[:, None])).astype(jnp.int32), axis=1)
    bins = jnp.arange(n_dst, dtype=jnp.int32)
    counts = jnp.sum(((dst[:, None] == bins[None, :]) & live[:, None]).astype(jnp.int32), axis=0)
    pairs = (counts + 1) // 2
    start = jnp.sum(jnp.where(bins[None, :] < dst[:, None], pairs[None, :], 0), axis=1)
    place = jnp.where(live, 2 * start + rank, -1)
    places = jnp.arange(2 * room, dtype=jnp.int32)
    hit = place[None, :] == places[:, None]
    slot_at = jnp.sum(jnp.where(hit, index[None, :], 0), axis=1)
    src_at = n_src + jnp.sum(jnp.where(hit, src[None, :] - n_src, 0), axis=1)
    dst_at = jnp.sum(jnp.where(hit, dst[None, :], 0), axis=1)[::2]
    steps = (jnp.sum(pairs) + UNROLL - 1) // UNROLL
    return jnp.concatenate([slot_at, src_at, dst_at, steps.reshape(1)])


def from_ring(value, axis, stride, size, shift):
    pairs = []
    for i in range(size):
        at = i // stride % RING
        pairs.append((i + ((at + shift) % RING - at) * stride, i))
    return lax.ppermute(value, axis, pairs)


def other_core(value):
    return lax.ppermute(value, "rep", [(i, i ^ 1) for i in range(RING * CORES)])


def shards(
    features, weight, cotangent, row_mask, block_rows, block_cols, block_values, block_count
):
    rows_dev, width = features.shape
    n_rep = lax.axis_size("rep")
    n_row = lax.axis_size("row")
    factor = 1.0 / math.sqrt(rows_dev * n_row * n_rep)
    group_blocks = n_rep * rows_dev // EDGE
    line_blocks = n_row * rows_dev // EDGE
    half_rows = rows_dev // 2
    per_half = half_rows // EDGE
    per_dev = rows_dev // EDGE
    i, j = lax.axis_index("row"), lax.axis_index("rep")
    z, x, y, core = i // RING, i % RING, j // CORES, j % CORES
    ring_x = functools.partial(from_ring, axis="row", stride=1, size=n_row)
    ring_z = functools.partial(from_ring, axis="row", stride=RING, size=n_row)
    ring_y = functools.partial(from_ring, axis="rep", stride=CORES, size=n_rep)
    shifts = (1, 3, 2)

    def gather(value, ring):
        got = {s: ring(value, shift=s) for s in shifts}
        return [value, got[1], got[2], got[3]]

    first, second = features[:half_rows], features[half_rows:]
    first_x, second_z = gather(first, ring_x), gather(second, ring_z)
    block_rows, block_cols, first_x = lax.optimization_barrier((block_rows, block_cols, first_x))
    second_z = jnp.concatenate(second_z)
    middle = second_z.shape[0] // 2
    up, down = ring_x(second_z, shift=1), ring_x(second_z, shift=3)
    across_up, across_down = ring_x(up[:middle], shift=1), ring_x(down[middle:], shift=3)
    line = gather(jnp.concatenate(first_x), ring_z)
    line += [second_z, up, across_up, across_down, down]

    live = jnp.arange(block_rows.shape[0], dtype=jnp.int32) < block_count[0]
    dev, q = block_rows // per_dev, block_rows % per_dev
    dy = (dev // CORES - y) % RING
    across = (dev % CORES) ^ core
    row_at = (across * RING + dy) * per_dev + q
    dev, q = block_cols // per_dev, block_cols % per_dev
    dz, dx = (dev // RING - z) % RING, (dev % RING - x) % RING
    h = q // per_half
    zx, xz = dz * RING + dx, dx * RING + dz
    gathered_at = (h * n_row + jnp.where(h == 0, zx, xz)) * per_half + q % per_half
    scattered_at = (h * n_row + jnp.where(h == 0, xz, zx)) * per_half + q % per_half
    forward = pair_lists(live, row_at, gathered_at, group_blocks, line_blocks)
    backward = pair_lists(live, scattered_at, row_at, line_blocks, group_blocks)
    line, forward, backward = lax.optimization_barrier((line, forward, backward))

    def scatter(parts, ring):
        got = {s: ring(parts[s], shift=RING - s) for s in shifts}
        return parts[0] + got[1].astype(f32) + got[2].astype(f32) + got[3].astype(f32)

    def cut(value, rows):
        return [value[k * rows : (k + 1) * rows] for k in range(RING)]

    side = RING * rows_dev
    mine, others = spmm(forward, block_values, line, ((side, f32), (side, bf16)), False)
    others = other_core(others)
    chip = [a + b.astype(f32) for a, b in zip(cut(mine, rows_dev), cut(others, rows_dev))]
    summed = scatter(chip[:1] + [c.astype(bf16) for c in chip[1:]], ring_y)
    aggregated = summed.astype(bf16)
    pre = jnp.dot(aggregated, weight, preferred_element_type=f32)
    gate = jax.nn.sigmoid(pre)
    output = (pre * gate).astype(bf16)
    mask = row_mask.astype(f32)[:, None]
    slope = (cotangent.astype(f32) * mask * gate * (1.0 + pre * (1.0 - gate))).astype(bf16)
    back = jnp.dot(slope, weight.T, preferred_element_type=f32).astype(bf16)
    backs = gather(back, ring_y)


    weight_term = lax.dot_general(
        aggregated, slope, (((0,), (0,)), ((), ())), preferred_element_type=f32
    )

    def trade(value, axis):
        return lax.all_to_all(value, axis, 0, 0, tiled=True)

    strips = trade(weight_term.reshape(n_row, -1, width), "row")
    backs, strips = lax.optimization_barrier((backs, strips))
    backs += [other_core(jnp.concatenate(backs))]

    ring_rows = RING * half_rows
    part_rows = ring_rows // 2
    splits = ((ring_rows, f32),) + ((ring_rows, bf16),) * (RING - 1)
    splits += ((ring_rows, f32), (part_rows, f32), (part_rows, bf16), (part_rows, bf16))
    splits += ((part_rows, bf16), (part_rows, bf16), (part_rows, f32))
    parts = spmm(backward, block_values, backs, splits, True)

    def send(parts, ring):
        return {s: ring(parts[s], shift=RING - s) for s in shifts}

    def add(own, got):
        return own + got[1].astype(f32) + got[2].astype(f32) + got[3].astype(f32)

    near_first = send(parts[:RING], ring_x)
    own_z, up_a, up_b, across_a, across_b, down_a, down_b = parts[RING:]
    through_a, through_b = ring_z(across_a, shift=3), ring_z(across_b, shift=1)
    up = jnp.concatenate([(up_a + through_a.astype(f32)).astype(bf16), up_b])
    down = jnp.concatenate([down_a, (down_b + through_b.astype(f32)).astype(bf16)])

    up, down, strips = lax.optimization_barrier((up, down, strips))
    from_up, from_down = ring_z(up, shift=3), ring_z(down, shift=1)
    strip = jnp.sum(strips, axis=0) * factor
    strip = jnp.sum(trade(jnp.broadcast_to(strip[None], (n_rep, *strip.shape)), "rep"), axis=0)
    strips = trade(jnp.broadcast_to(strip[None], (n_row, *strip.shape)), "row")
    grad_weight = strips.reshape(-1, width)

    near_sum = cut(add(parts[0], near_first), half_rows)
    far_first = near_sum[:1] + [c.astype(bf16) for c in near_sum[1:]]
    far_first_got = send(far_first, ring_z)
    near_sum = cut(own_z + from_up.astype(f32) + from_down.astype(f32), half_rows)
    far_second = near_sum[:1] + [c.astype(bf16) for c in near_sum[1:]]
    far_second_got = send(far_second, ring_x)
    totals = [add(far_first[0], far_first_got), add(far_second[0], far_second_got)]
    grad_features = jnp.concatenate(totals).astype(bf16)
    return output, grad_features, grad_weight


def solution(mesh):
    in_specs = (
        P(("row", "rep"), None),
        P(),
        P(("row", "rep"), None),
        P(("row", "rep")),
        P(("row", "rep")),
        P(("row", "rep")),
        P(("row", "rep"), None, None),
        P(("row", "rep")),
    )
    out_specs = (P(("row", "rep"), None), P(("row", "rep"), None), P())
    return jax.shard_map(shards, mesh=mesh, in_specs=in_specs, out_specs=out_specs, check_vma=False)
```

```python
import functools
import math

import jax
import jax.numpy as jnp
from jax import lax
from jax.experimental import pallas as pl
from jax.experimental.pallas import tpu as pltpu
from jax.sharding import PartitionSpec as P

EDGE = 128
MIB = 2**20
RING = 4
CORES = 2
UNROLL = 16
DEPTH = 4

f32 = jnp.float32
bf16 = jnp.bfloat16


def spmm_body(transposed, splits, n_src, room, table, values, *refs):
    pieces, rest = refs[:n_src], refs[n_src:]
    outs, (src, acc, narrow, ring, src_sem, out_sem, sems) = rest[: len(splits)], rest[len(splits) :]
    n_steps = table[5 * room]

    def fetch(step, bank):
        for u in range(UNROLL):
            pair = step * UNROLL + u
            for half in range(2):
                place = pl.ds(half * EDGE, EDGE)
                at = ring.at[bank, u, place, :] if transposed else ring.at[bank, u, :, place]
                pltpu.make_async_copy(values.at[table[2 * pair + half]], at, sems.at[bank]).start()

    for ahead in range(DEPTH - 1):

        @pl.when(ahead < n_steps)
        def _():
            fetch(ahead, ahead)

    base = 0
    for piece in pieces:
        rows = piece.shape[0]
        pltpu.make_async_copy(piece, src.at[pl.ds(base, rows), :], src_sem).start()
        base += rows
    src[pl.ds(base, EDGE), :] = jnp.zeros((EDGE, src.shape[1]), src.dtype)
    acc[...] = jnp.zeros_like(acc)
    loaded = src.at[pl.ds(0, base), :]
    pltpu.make_async_copy(loaded, loaded, src_sem).wait()
    dims = (((0,), (0,)), ((), ())) if transposed else (((1,), (0,)), ((), ()))

    def step(t, carry):
        bank = lax.rem(t, DEPTH)
        ahead = t + DEPTH - 1

        @pl.when(ahead < n_steps)
        def _():
            fetch(ahead, lax.rem(ahead, DEPTH))

        pltpu.make_async_copy(ring.at[bank], ring.at[bank], sems.at[bank]).wait()
        for u in range(UNROLL):
            pair = t * UNROLL + u
            x = jnp.concatenate(
                [
                    src[pl.ds(pl.multiple_of(table[2 * (room + pair) + half] * EDGE, EDGE), EDGE), :]
                    for half in range(2)
                ],
                axis=0,
            )
            product = lax.dot_general(ring[bank, u], x, dims, preferred_element_type=f32)
            acc[pl.ds(pl.multiple_of(table[4 * room + pair] * EDGE, EDGE), EDGE), :] += product
        return carry

    lax.fori_loop(0, n_steps, step, 0)
    base = 0
    for out in outs:
        rows = out.shape[0]
        at = acc.at[pl.ds(base, rows), :]
        if out.dtype != acc.dtype:
            narrow[pl.ds(base, rows), :] = acc[pl.ds(base, rows), :].astype(out.dtype)
            at = narrow.at[pl.ds(base, rows), :]
        pltpu.make_async_copy(at, out, out_sem).start()
        base += rows
    for out in outs:
        pltpu.make_async_copy(out, out, out_sem).wait()


def spmm(table, values, pieces, splits, transposed):
    width = pieces[0].shape[1]
    n_src = sum(p.shape[0] for p in pieces)
    n_dst = sum(rows for rows, _ in splits)
    bank = (UNROLL, 2 * EDGE, EDGE) if transposed else (UNROLL, EDGE, 2 * EDGE)
    smem = pl.BlockSpec(memory_space=pltpu.SMEM)
    anywhere = pl.BlockSpec(memory_space=pl.ANY)
    return pl.pallas_call(
        functools.partial(spmm_body, transposed, splits, len(pieces), table.shape[0] // 5),
        in_specs=[smem] + [anywhere] * (1 + len(pieces)),
        out_specs=[anywhere] * len(splits),
        out_shape=[jax.ShapeDtypeStruct((rows, width), kind) for rows, kind in splits],
        scratch_shapes=[
            pltpu.VMEM((n_src + EDGE, width), bf16),
            pltpu.VMEM((n_dst, width), f32),
            pltpu.VMEM((n_dst, width), bf16),
            pltpu.VMEM((DEPTH, *bank), bf16),
            pltpu.SemaphoreType.DMA,
            pltpu.SemaphoreType.DMA,
            pltpu.SemaphoreType.DMA((DEPTH,)),
        ],
        compiler_params=pltpu.CompilerParams(vmem_limit_bytes=45 * MIB),
        cost_estimate=pl.CostEstimate(
            flops=2 * values.shape[0] * EDGE * EDGE * width,
            bytes_accessed=2 * values.shape[0] * EDGE * EDGE,
            transcendentals=0,
        ),
    )(table, values, *pieces)


def pair_lists(live, dst, src, n_dst, n_src):
    slots = dst.shape[0]
    room = -(-((slots + n_dst) // 2) // UNROLL) * UNROLL
    index = jnp.arange(slots, dtype=jnp.int32)
    same = (dst[:, None] == dst[None, :]) & live[None, :]
    rank = jnp.sum((same & (index[None, :] < index[:, None])).astype(jnp.int32), axis=1)
    bins = jnp.arange(n_dst, dtype=jnp.int32)
    counts = jnp.sum(((dst[:, None] == bins[None, :]) & live[:, None]).astype(jnp.int32), axis=0)
    pairs = (counts + 1) // 2
    start = jnp.sum(jnp.where(bins[None, :] < dst[:, None], pairs[None, :], 0), axis=1)
    place = jnp.where(live, 2 * start + rank, -1)
    places = jnp.arange(2 * room, dtype=jnp.int32)
    hit = place[None, :] == places[:, None]
    slot_at = jnp.sum(jnp.where(hit, index[None, :], 0), axis=1)
    src_at = n_src + jnp.sum(jnp.where(hit, src[None, :] - n_src, 0), axis=1)
    dst_at = jnp.sum(jnp.where(hit, dst[None, :], 0), axis=1)[::2]
    steps = (jnp.sum(pairs) + UNROLL - 1) // UNROLL
    return jnp.concatenate([slot_at, src_at, dst_at, steps.reshape(1)])


def from_ring(value, axis, stride, size, shift):
    pairs = []
    for i in range(size):
        at = i // stride % RING
        pairs.append((i + ((at + shift) % RING - at) * stride, i))
    return lax.ppermute(value, axis, pairs)


def other_core(value):
    return lax.ppermute(value, "rep", [(i, i ^ 1) for i in range(RING * CORES)])


def shards(
    features, weight, cotangent, row_mask, block_rows, block_cols, block_values, block_count
):
    rows_dev, width = features.shape
    n_rep = lax.axis_size("rep")
    n_row = lax.axis_size("row")
    factor = 1.0 / math.sqrt(rows_dev * n_row * n_rep)
    group_blocks = n_rep * rows_dev // EDGE
    line_blocks = n_row * rows_dev // EDGE
    half_rows = rows_dev // 2
    per_half = half_rows // EDGE
    per_dev = rows_dev // EDGE
    i, j = lax.axis_index("row"), lax.axis_index("rep")
    z, x, y, core = i // RING, i % RING, j // CORES, j % CORES
    ring_x = functools.partial(from_ring, axis="row", stride=1, size=n_row)
    ring_z = functools.partial(from_ring, axis="row", stride=RING, size=n_row)
    ring_y = functools.partial(from_ring, axis="rep", stride=CORES, size=n_rep)
    shifts = (1, 3, 2)

    def gather(value, ring):
        got = {s: ring(value, shift=s) for s in shifts}
        return [value, got[1], got[2], got[3]]

    first, second = features[:half_rows], features[half_rows:]
    first_x, second_z = gather(first, ring_x), gather(second, ring_z)
    block_rows, block_cols, first_x = lax.optimization_barrier((block_rows, block_cols, first_x))
    second_z = jnp.concatenate(second_z)
    middle = second_z.shape[0] // 2
    up, down = ring_x(second_z, shift=1), ring_x(second_z, shift=3)
    across_up, across_down = ring_x(up[:middle], shift=1), ring_x(down[middle:], shift=3)
    line = gather(jnp.concatenate(first_x), ring_z)
    line += [second_z, up, across_up, across_down, down]

    live = jnp.arange(block_rows.shape[0], dtype=jnp.int32) < block_count[0]
    dev, q = block_rows // per_dev, block_rows % per_dev
    dy = (dev // CORES - y) % RING
    across = (dev % CORES) ^ core
    row_at = (across * RING + dy) * per_dev + q
    dev, q = block_cols // per_dev, block_cols % per_dev
    dz, dx = (dev // RING - z) % RING, (dev % RING - x) % RING
    h = q // per_half
    zx, xz = dz * RING + dx, dx * RING + dz
    gathered_at = (h * n_row + jnp.where(h == 0, zx, xz)) * per_half + q % per_half
    scattered_at = (h * n_row + jnp.where(h == 0, xz, zx)) * per_half + q % per_half
    forward = pair_lists(live, row_at, gathered_at, group_blocks, line_blocks)
    backward = pair_lists(live, scattered_at, row_at, line_blocks, group_blocks)
    line, forward, backward = lax.optimization_barrier((line, forward, backward))

    def scatter(parts, ring):
        got = {s: ring(parts[s], shift=RING - s) for s in shifts}
        return parts[0] + got[1].astype(f32) + got[2].astype(f32) + got[3].astype(f32)

    def cut(value, rows):
        return [value[k * rows : (k + 1) * rows] for k in range(RING)]

    side = RING * rows_dev
    mine, others = spmm(forward, block_values, line, ((side, f32), (side, bf16)), False)
    others = other_core(others)
    chip = [a + b.astype(f32) for a, b in zip(cut(mine, rows_dev), cut(others, rows_dev))]
    summed = scatter(chip[:1] + [c.astype(bf16) for c in chip[1:]], ring_y)
    aggregated = summed.astype(bf16)
    pre = jnp.dot(aggregated, weight, preferred_element_type=f32)
    gate = jax.nn.sigmoid(pre)
    output = (pre * gate).astype(bf16)
    mask = row_mask.astype(f32)[:, None]
    slope = (cotangent.astype(f32) * mask * gate * (1.0 + pre * (1.0 - gate))).astype(bf16)
    back = jnp.dot(slope, weight.T, preferred_element_type=f32).astype(bf16)
    backs = gather(back, ring_y)


    weight_term = lax.dot_general(
        aggregated, slope, (((0,), (0,)), ((), ())), preferred_element_type=f32
    )

    def trade(value, axis):
        return lax.all_to_all(value, axis, 0, 0, tiled=True)

    strips = trade(weight_term.reshape(n_row, -1, width), "row")
    backs, strips = lax.optimization_barrier((backs, strips))
    backs += [other_core(jnp.concatenate(backs))]

    ring_rows = RING * half_rows
    part_rows = ring_rows // 2
    splits = ((ring_rows, f32),) + ((ring_rows, bf16),) * (RING - 1)
    splits += ((ring_rows, f32), (part_rows, f32), (part_rows, bf16), (part_rows, bf16))
    splits += ((part_rows, bf16), (part_rows, bf16), (part_rows, f32))
    parts = spmm(backward, block_values, backs, splits, True)

    def send(parts, ring):
        return {s: ring(parts[s], shift=RING - s) for s in shifts}

    def add(own, got):
        return own + got[1].astype(f32) + got[2].astype(f32) + got[3].astype(f32)

    near_first = send(parts[:RING], ring_x)
    own_z, up_a, up_b, across_a, across_b, down_a, down_b = parts[RING:]
    through_a, through_b = ring_z(across_a, shift=3), ring_z(across_b, shift=1)
    up = jnp.concatenate([(up_a + through_a.astype(f32)).astype(bf16), up_b])
    down = jnp.concatenate([down_a, (down_b + through_b.astype(f32)).astype(bf16)])

    up, down, strips = lax.optimization_barrier((up, down, strips))
    from_up, from_down = ring_z(up, shift=3), ring_z(down, shift=1)
    strip = jnp.sum(strips, axis=0)
    strip = jnp.sum(trade(jnp.broadcast_to(strip[None], (n_rep, *strip.shape)), "rep"), axis=0)
    grad_weight = trade(jnp.broadcast_to(strip[None], (n_row, *strip.shape)), "row")

    far_first = cut(add(parts[0], near_first).astype(bf16), half_rows)
    far_first_got = send(far_first, ring_z)
    far_second = own_z + from_up.astype(f32) + from_down.astype(f32)
    far_second = cut(far_second.astype(bf16), half_rows)
    far_second_got = send(far_second, ring_x)
    grad_weight, far_second_got = lax.optimization_barrier((grad_weight, far_second_got))
    grad_weight = grad_weight.reshape(-1, width) * factor
    totals = [add(far_first[0], far_first_got), add(far_second[0], far_second_got)]
    grad_features = jnp.concatenate(totals).astype(bf16)
    return output, grad_features, grad_weight


def solution(mesh):
    in_specs = (
        P(("row", "rep"), None),
        P(),
        P(("row", "rep"), None),
        P(("row", "rep")),
        P(("row", "rep")),
        P(("row", "rep")),
        P(("row", "rep"), None, None),
        P(("row", "rep")),
    )
    out_specs = (P(("row", "rep"), None), P(("row", "rep"), None), P())
    return jax.shard_map(shards, mesh=mesh, in_specs=in_specs, out_specs=out_specs, check_vma=False)
```

```python
import functools
import math

import jax
import jax.numpy as jnp
from jax import lax
from jax.experimental import pallas as pl
from jax.experimental.pallas import tpu as pltpu
from jax.sharding import PartitionSpec as P

EDGE = 128
MIB = 2**20
RING = 4
CORES = 2
UNROLL = 16
DEPTH = 4

f32 = jnp.float32
bf16 = jnp.bfloat16


def spmm_body(transposed, splits, n_src, room, table, values, *refs):
    pieces, rest = refs[:n_src], refs[n_src:]
    outs, (src, acc, narrow, ring, src_sem, out_sem, sems) = rest[: len(splits)], rest[len(splits) :]
    n_steps = table[5 * room]

    def fetch(step, bank):
        for u in range(UNROLL):
            pair = step * UNROLL + u
            for half in range(2):
                place = pl.ds(half * EDGE, EDGE)
                at = ring.at[bank, u, place, :] if transposed else ring.at[bank, u, :, place]
                pltpu.make_async_copy(values.at[table[2 * pair + half]], at, sems.at[bank]).start()

    for ahead in range(DEPTH - 1):

        @pl.when(ahead < n_steps)
        def _():
            fetch(ahead, ahead)

    base = 0
    for piece in pieces:
        rows = piece.shape[0]
        pltpu.make_async_copy(piece, src.at[pl.ds(base, rows), :], src_sem).start()
        base += rows
    src[pl.ds(base, EDGE), :] = jnp.zeros((EDGE, src.shape[1]), src.dtype)
    acc[...] = jnp.zeros_like(acc)
    loaded = src.at[pl.ds(0, base), :]
    pltpu.make_async_copy(loaded, loaded, src_sem).wait()
    dims = (((0,), (0,)), ((), ())) if transposed else (((1,), (0,)), ((), ()))

    def step(t, carry):
        bank = lax.rem(t, DEPTH)
        ahead = t + DEPTH - 1

        @pl.when(ahead < n_steps)
        def _():
            fetch(ahead, lax.rem(ahead, DEPTH))

        pltpu.make_async_copy(ring.at[bank], ring.at[bank], sems.at[bank]).wait()
        for u in range(UNROLL):
            pair = t * UNROLL + u
            x = jnp.concatenate(
                [
                    src[pl.ds(pl.multiple_of(table[2 * (room + pair) + half] * EDGE, EDGE), EDGE), :]
                    for half in range(2)
                ],
                axis=0,
            )
            product = lax.dot_general(ring[bank, u], x, dims, preferred_element_type=f32)
            acc[pl.ds(pl.multiple_of(table[4 * room + pair] * EDGE, EDGE), EDGE), :] += product
        return carry

    lax.fori_loop(0, n_steps, step, 0)
    base = 0
    for out in outs:
        rows = out.shape[0]
        at = acc.at[pl.ds(base, rows), :]
        if out.dtype != acc.dtype:
            narrow[pl.ds(base, rows), :] = acc[pl.ds(base, rows), :].astype(out.dtype)
            at = narrow.at[pl.ds(base, rows), :]
        pltpu.make_async_copy(at, out, out_sem).start()
        base += rows
    for out in outs:
        pltpu.make_async_copy(out, out, out_sem).wait()


def spmm(table, values, pieces, splits, transposed):
    width = pieces[0].shape[1]
    n_src = sum(p.shape[0] for p in pieces)
    n_dst = sum(rows for rows, _ in splits)
    bank = (UNROLL, 2 * EDGE, EDGE) if transposed else (UNROLL, EDGE, 2 * EDGE)
    smem = pl.BlockSpec(memory_space=pltpu.SMEM)
    anywhere = pl.BlockSpec(memory_space=pl.ANY)
    return pl.pallas_call(
        functools.partial(spmm_body, transposed, splits, len(pieces), table.shape[0] // 5),
        in_specs=[smem] + [anywhere] * (1 + len(pieces)),
        out_specs=[anywhere] * len(splits),
        out_shape=[jax.ShapeDtypeStruct((rows, width), kind) for rows, kind in splits],
        scratch_shapes=[
            pltpu.VMEM((n_src + EDGE, width), bf16),
            pltpu.VMEM((n_dst, width), f32),
            pltpu.VMEM((n_dst, width), bf16),
            pltpu.VMEM((DEPTH, *bank), bf16),
            pltpu.SemaphoreType.DMA,
            pltpu.SemaphoreType.DMA,
            pltpu.SemaphoreType.DMA((DEPTH,)),
        ],
        compiler_params=pltpu.CompilerParams(vmem_limit_bytes=45 * MIB),
        cost_estimate=pl.CostEstimate(
            flops=2 * values.shape[0] * EDGE * EDGE * width,
            bytes_accessed=2 * values.shape[0] * EDGE * EDGE,
            transcendentals=0,
        ),
    )(table, values, *pieces)


def pair_lists(live, n_dst, dst, src, n_src):
    slots = dst.shape[0]
    room = -(-((slots + n_dst) // 2) // UNROLL) * UNROLL
    index = jnp.arange(slots, dtype=jnp.int32)
    same = (dst[:, None] == dst[None, :]) & live[None, :]
    rank = jnp.sum((same & (index[None, :] < index[:, None])).astype(jnp.int32), axis=1)
    bins = jnp.arange(n_dst, dtype=jnp.int32)
    counts = jnp.sum(((dst[:, None] == bins[None, :]) & live[:, None]).astype(jnp.int32), axis=0)
    pairs = (counts + 1) // 2
    start = jnp.sum(jnp.where(bins[None, :] < dst[:, None], pairs[None, :], 0), axis=1)
    place = jnp.where(live, 2 * start + rank, -1)
    places = jnp.arange(2 * room, dtype=jnp.int32)
    hit = place[None, :] == places[:, None]
    slot_at = jnp.sum(jnp.where(hit, index[None, :], 0), axis=1)
    src_at = n_src + jnp.sum(jnp.where(hit, src[None, :] - n_src, 0), axis=1)
    dst_at = jnp.sum(jnp.where(hit, dst[None, :], 0), axis=1)[::2]
    steps = (jnp.sum(pairs) + UNROLL - 1) // UNROLL
    return jnp.concatenate([slot_at, src_at, dst_at, steps.reshape(1)])


def from_ring(value, axis, stride, size, shift):
    pairs = []
    for i in range(size):
        at = i // stride % RING
        pairs.append((i + ((at + shift) % RING - at) * stride, i))
    return lax.ppermute(value, axis, pairs)


def other_core(value):
    return lax.ppermute(value, "rep", [(i, i ^ 1) for i in range(RING * CORES)])


def shards(
    features, weight, cotangent, row_mask, block_rows, block_cols, block_values, block_count
):
    rows_dev, width = features.shape
    n_rep = lax.axis_size("rep")
    n_row = lax.axis_size("row")
    factor = 1.0 / math.sqrt(rows_dev * n_row * n_rep)
    group_blocks = n_rep * rows_dev // EDGE
    line_blocks = n_row * rows_dev // EDGE
    half_rows = rows_dev // 2
    per_half = half_rows // EDGE
    per_dev = rows_dev // EDGE
    i, j = lax.axis_index("row"), lax.axis_index("rep")
    z, x, y, core = i // RING, i % RING, j // CORES, j % CORES
    ring_x = functools.partial(from_ring, axis="row", stride=1, size=n_row)
    ring_z = functools.partial(from_ring, axis="row", stride=RING, size=n_row)
    ring_y = functools.partial(from_ring, axis="rep", stride=CORES, size=n_rep)
    shifts = (1, 3, 2)

    def gather(value, ring):
        got = {s: ring(value, shift=s) for s in shifts}
        return [value, got[1], got[2], got[3]]

    first, second = features[:half_rows], features[half_rows:]
    first_x, second_z = gather(first, ring_x), gather(second, ring_z)
    block_rows, block_cols, first_x = lax.optimization_barrier((block_rows, block_cols, first_x))
    second_z = jnp.concatenate(second_z)
    middle = second_z.shape[0] // 2
    up, down = ring_x(second_z, shift=1), ring_x(second_z, shift=3)
    across_up, across_down = ring_x(up[:middle], shift=1), ring_x(down[middle:], shift=3)
    line = gather(jnp.concatenate(first_x), ring_z)
    line += [second_z, up, across_up, across_down, down]

    live = jnp.arange(block_rows.shape[0], dtype=jnp.int32) < block_count[0]
    dev, q = block_rows // per_dev, block_rows % per_dev
    dy = (dev // CORES - y) % RING
    across = (dev % CORES) ^ core
    row_at = (across * RING + dy) * per_dev + q
    dev, q = block_cols // per_dev, block_cols % per_dev
    dz, dx = (dev // RING - z) % RING, (dev % RING - x) % RING
    h = q // per_half
    zx, xz = dz * RING + dx, dx * RING + dz
    gathered_at = (h * n_row + jnp.where(h == 0, zx, xz)) * per_half + q % per_half
    scattered_at = (h * n_row + jnp.where(h == 0, xz, zx)) * per_half + q % per_half
    tables = jax.vmap(functools.partial(pair_lists, live, max(group_blocks, line_blocks)))(
        jnp.stack([row_at, scattered_at]),
        jnp.stack([gathered_at, row_at]),
        jnp.array([line_blocks, group_blocks], jnp.int32),
    )
    line, forward, backward = lax.optimization_barrier((line, tables[0], tables[1]))

    def scatter(parts, ring):
        got = {s: ring(parts[s], shift=RING - s) for s in shifts}
        return parts[0] + got[1].astype(f32) + got[2].astype(f32) + got[3].astype(f32)

    def cut(value, rows):
        return [value[k * rows : (k + 1) * rows] for k in range(RING)]

    side = RING * rows_dev
    mine, others = spmm(forward, block_values, line, ((side, f32), (side, bf16)), False)
    others = other_core(others)
    chip = [a + b.astype(f32) for a, b in zip(cut(mine, rows_dev), cut(others, rows_dev))]
    summed = scatter(chip[:1] + [c.astype(bf16) for c in chip[1:]], ring_y)
    aggregated = summed.astype(bf16)
    pre = jnp.dot(aggregated, weight, preferred_element_type=f32)
    gate = jax.nn.sigmoid(pre)
    output = (pre * gate).astype(bf16)
    mask = row_mask.astype(f32)[:, None]
    slope = (cotangent.astype(f32) * mask * gate * (1.0 + pre * (1.0 - gate))).astype(bf16)
    back = jnp.dot(slope, weight.T, preferred_element_type=f32).astype(bf16)
    backs = gather(back, ring_y)


    weight_term = lax.dot_general(
        aggregated, slope, (((0,), (0,)), ((), ())), preferred_element_type=f32
    )

    def trade(value, axis):
        return lax.all_to_all(value, axis, 0, 0, tiled=True)

    strips = trade(weight_term.reshape(n_row, -1, width), "row")
    backs, strips = lax.optimization_barrier((backs, strips))
    backs += [other_core(jnp.concatenate(backs))]

    ring_rows = RING * half_rows
    part_rows = ring_rows // 2
    splits = ((ring_rows, f32),) + ((ring_rows, bf16),) * (RING - 1)
    splits += ((ring_rows, f32), (part_rows, f32), (part_rows, bf16), (part_rows, bf16))
    splits += ((part_rows, bf16), (part_rows, bf16), (part_rows, f32))
    parts = spmm(backward, block_values, backs, splits, True)

    def send(parts, ring):
        return {s: ring(parts[s], shift=RING - s) for s in shifts}

    def add(own, got):
        return own + got[1].astype(f32) + got[2].astype(f32) + got[3].astype(f32)

    near_first = send(parts[:RING], ring_x)
    own_z, up_a, up_b, across_a, across_b, down_a, down_b = parts[RING:]
    through_a, through_b = ring_z(across_a, shift=3), ring_z(across_b, shift=1)
    up = jnp.concatenate([(up_a + through_a.astype(f32)).astype(bf16), up_b])
    down = jnp.concatenate([down_a, (down_b + through_b.astype(f32)).astype(bf16)])

    up, down, strips = lax.optimization_barrier((up, down, strips))
    from_up, from_down = ring_z(up, shift=3), ring_z(down, shift=1)
    strip = jnp.sum(strips, axis=0)
    strip = jnp.sum(trade(jnp.broadcast_to(strip[None], (n_rep, *strip.shape)), "rep"), axis=0)
    grad_weight = trade(jnp.broadcast_to(strip[None], (n_row, *strip.shape)), "row")

    far_first = cut(add(parts[0], near_first).astype(bf16), half_rows)
    far_first_got = send(far_first, ring_z)
    far_second = own_z + from_up.astype(f32) + from_down.astype(f32)
    far_second = cut(far_second.astype(bf16), half_rows)
    far_second_got = send(far_second, ring_x)
    grad_weight, far_second_got = lax.optimization_barrier((grad_weight, far_second_got))
    grad_weight = grad_weight.reshape(-1, width) * factor
    totals = [add(far_first[0], far_first_got), add(far_second[0], far_second_got)]
    grad_features = jnp.concatenate(totals).astype(bf16)
    return output, grad_features, grad_weight


def solution(mesh):
    in_specs = (
        P(("row", "rep"), None),
        P(),
        P(("row", "rep"), None),
        P(("row", "rep")),
        P(("row", "rep")),
        P(("row", "rep")),
        P(("row", "rep"), None, None),
        P(("row", "rep")),
    )
    out_specs = (P(("row", "rep"), None), P(("row", "rep"), None), P())
    return jax.shard_map(shards, mesh=mesh, in_specs=in_specs, out_specs=out_specs, check_vma=False)
```
